128 devices in a mesh: row: 8 (over x_lo, y), col: 16 (over x_hi, z, core).
Axes of the slice: x: 4 (x_hi: 2, x_lo: 2; x = x_hi * 2 + x_lo), y: 4, z: 4, core: 2. Of those that a mesh axis runs over, the one named last changes fastest.
Arguments:
- out_grad: bfloat16 [1024, 6144], P('row', 'col'), may hold values from -6 to 6
- hidden: bfloat16 [1024, 24576], P('row'), may hold values from -0.1796875 to 0.1796875
- weight: bfloat16 [24576, 6144], P('row', 'col'), may hold values from -0.078125 to 0.078125
- compress: bfloat16 [512, 128], replicated, may hold values from -0.25 to 0.25
- feedback: bfloat16 [16, 1024, 24576], P('col', None, 'row'), may hold values from -1.5 to 1.5
Outputs:
- grad_input: bfloat16 [1024, 24576], P('col', 'row')
- grad_weight: bfloat16 [24576, 6144], P('row', 'col')
- new_feedback: bfloat16 [16, 1024, 24576], P('col', None, 'row')
The draws below stay inside these ranges and needn't reach their ends.
All inputs are finite; a program needn't handle non-finite values.
Results may differ from the reference program's by a relative error of at most 0.0056.
Values may be sent and summed in bfloat16 or wider, within the bound.
A program may use at most 256 MiB of HBM per device.

```python
import jax
import jax.numpy as jnp
from jax import lax

D = 6144
FF = 24576
BLK = 512
SUB = 128
TOKENS = 1024
N_COL = 16


def strengthened(array, key, source, target, blocks, factor):
    def block_of(axis_at):
        return (jnp.arange(array.shape[axis_at]) // (array.shape[axis_at] // blocks)).reshape((-1,) + (1,) * (array.ndim - 1 - axis_at))

    near = jax.random.permutation(key, blocks)[block_of(target)]
    other_side = (block_of(target) + blocks // 2) % blocks
    return jnp.where((block_of(source) == near) | (block_of(source) == other_side), factor * array, array)


def block_levels(key, dims, cuts, least, top_value):
    def one(dim, shards_of):
        steps = jax.random.uniform(jax.random.fold_in(jax.random.fold_in(key, 6), dim), (shards_of,), jnp.float32, least / len(cuts), top_value / len(cuts))
        return jnp.repeat(jnp.exp(steps), dims[dim] // shards_of).reshape((-1,) + (1,) * (len(dims) - dim - 1))

    loudness = one(*cuts[0])
    for cut in cuts[1:]:
        loudness = loudness * one(*cut)
    return loudness


def bell_draw(stream_key, dims, scale, most, split=(), held_as=jnp.bfloat16):
    array = jax.random.normal(stream_key, dims, jnp.float32) * scale
    if len(split) > 0:
        array = block_levels(stream_key, dims, split, -0.22, 0.18) * array
    return jnp.clip(array, min=-most, max=most).astype(held_as)


def heavy_noise(stream_key, dims, deviation, bound, pieces, heavy, held_as=jnp.bfloat16):
    array = deviation * jax.random.normal(stream_key, dims, jnp.float32)
    if pieces:
        array = array * block_levels(stream_key, dims, pieces, -0.22, 0.18)
    return jnp.clip(strengthened(array, jax.random.fold_in(stream_key, 3), *heavy), -bound, bound).astype(held_as)


def setup_inputs(seed: int = 0) -> dict:
    arg_keys = jax.random.split(jax.random.key(seed), 6)
    return {
        "out_grad": bell_draw(arg_keys[0], (TOKENS, D), 1.0, 6.0, ((0, 8), (1, 16))),
        "hidden": heavy_noise(arg_keys[1], (TOKENS, FF), 0.03, 0.1796875, ((0, 8),), (0, 1, 8, 2.0)),
        "weight": bell_draw(arg_keys[2], (FF, D), D ** -0.5, 0.078125, ((0, 8), (1, 16))),
        "compress": bell_draw(arg_keys[3], (BLK, SUB), BLK ** -0.5, 0.25),
        "feedback": bell_draw(arg_keys[4], (N_COL, TOKENS, FF), 0.25, 1.5, ((0, 16), (2, 8))),
    }


def reference(out_grad, hidden, weight, compress, feedback):
    width = D // N_COL
    weight_cols = weight.reshape(FF, N_COL, width).transpose(1, 0, 2)
    grad_cols = out_grad.reshape(TOKENS, N_COL, width).transpose(1, 0, 2)
    comp = compress.astype(jnp.float32)

    def one_col(total, inputs):
        grads, wcols, resid = inputs
        partial_value = lax.dot_general(grads, wcols, (((1,), (1,)), ((), ())), preferred_element_type=jnp.float32)
        acc = partial_value + resid.astype(jnp.float32)
        blocks = acc.astype(jnp.bfloat16).astype(jnp.float32).reshape(TOKENS, FF // BLK, BLK)
        code = jnp.einsum('tnb,bs->tns', blocks, comp)
        code_low = code.astype(jnp.bfloat16).astype(jnp.float32)
        recon = jnp.einsum('tns,bs->tnb', code_low, comp).reshape(TOKENS, FF)
        fresh = (acc - recon).astype(jnp.bfloat16)
        return total + code, fresh

    start = jnp.zeros((TOKENS, FF // BLK, SUB), jnp.float32)
    total, new_feedback = lax.scan(one_col, start, (grad_cols, weight_cols, feedback))
    total_low = total.astype(jnp.bfloat16).astype(jnp.float32)
    grad_input = jnp.einsum('tns,bs->tnb', total_low, comp).reshape(TOKENS, FF).astype(jnp.bfloat16)
    grad_weight = jnp.dot(hidden.T, out_grad, preferred_element_type=jnp.float32).astype(jnp.bfloat16)
    return grad_input, grad_weight, new_feedback
```

```python
import jax
import jax.numpy as jnp
from jax import lax
from jax.experimental import pallas as pl
from jax.experimental.pallas import tpu as pltpu
from jax.sharding import PartitionSpec as P

MESH = pl.DeviceIdType.MESH
NT = (((1,), (1,)), ((), ()))
NN = (((1,), (0,)), ((), ()))
F32 = jnp.float32
BF16 = jnp.bfloat16

SLOTS = [(0, 0), (1, 0), (0, 1), (0, 3), (0, 2), (1, 1), (1, 3), (1, 2)]
POS = {slot: i for i, slot in enumerate(SLOTS)}
CHUNK = 384


def dot(a, b, dims):
    return lax.dot_general(a, b, dims, preferred_element_type=F32)


def body(og_ref, hidden, weight, comp_ref, feedback, gi_ref, gw_ref, nf_ref,
         og_all, og_t, w_buf, fbuf, hid, cbuf, pbuf, csend, cx, ksum, cs2, cz, tot,
         g_s, g_r, hy_s, hy_r, hx_s, hx_r, hz_s, hz_r, hc_s, hc_r,
         p_s, p_r, cx_s, cx_r, cz_s, cz_r, w_sem, f_sem, own_sem):
    row = lax.axis_index("row")
    col = lax.axis_index("col")
    x_lo, y = row // 4, row % 4
    core, z, x_hi = col % 2, (col // 2) % 4, col // 8
    x = x_hi * 2 + x_lo

    def dev(dx, dy, dz, dc):
        xx, yy, zz, cc = (x + dx + 4) % 4, (y + dy + 4) % 4, (z + dz + 4) % 4, (core + dc) % 2
        return ((xx % 2) * 4 + yy, ((xx // 2) * 4 + zz) * 2 + cc)

    x_pair = 1 - 2 * x_lo
    z_steps = (1 - 2 * (z % 2), 2 * (z % 2) - 1)
    par = z % 2

    barrier = pltpu.get_barrier_semaphore()
    peers = [dev(0, 1, 0, 0), dev(0, -1, 0, 0), dev(0, 2, 0, 0)]
    peers += [dev(n, a, 0, 0) for n in (1, -1) for a in (0, 1, -1, 2)]
    peers += [dev(0, 0, 1, 0), dev(0, 0, -1, 0), dev(0, 0, 2, 0), dev(2, 0, 0, 0), dev(0, 0, 0, 1)]
    for peer in peers:
        pl.semaphore_signal(barrier, inc=1, device_id=peer, device_id_type=MESH)

    def row_of(slot):
        dx, dy = slot
        xl = x_lo if dx == 0 else 1 - x_lo
        return xl * 4 + (y + dy) % 4

    w_copy = pltpu.make_async_copy(weight, w_buf, w_sem)
    w_copy.start()
    f_copies = []
    for i, slot in enumerate(SLOTS):
        start = pl.multiple_of(row_of(slot) * 128, 128)
        cp = pltpu.make_async_copy(feedback.at[0, pl.ds(start, 128), :], fbuf.at[i], f_sem.at[i])
        cp.start()
        f_copies.append(cp)
    og_all[0] = og_ref[...]
    own_copies = []
    for k in range(8):
        start = pl.multiple_of(row * 3072 + k * CHUNK, 128)
        cp = pltpu.make_async_copy(hidden.at[:, pl.ds(start, CHUNK)], hid.at[k, 0], own_sem.at[k])
        cp.start()
        own_copies.append(cp)

    pl.semaphore_wait(barrier, len(peers))

    sends = []

    def send(src, dst, s_sem, r_sem, to):
        cp = pltpu.make_async_remote_copy(src_ref=src, dst_ref=dst, send_sem=s_sem, recv_sem=r_sem,
                                          device_id=to, device_id_type=MESH)
        cp.start()
        sends.append(cp)
        return cp

    def arrived(dst, sem):
        pltpu.make_async_copy(dst, dst, sem).wait()

    i = POS[1, 0]
    send(og_ref, og_all.at[i], g_s.at[0], g_r.at[i], dev(x_pair, 0, 0, 0))
    for n, a in enumerate((1, -1, 2)):
        i = POS[0, (-a) % 4]
        send(og_ref, og_all.at[i], g_s.at[1 + n], g_r.at[i], dev(0, a, 0, 0))

    def chunk_of(p, t, c):
        return p * 4 + t * 2 + c

    def cols(r, k):
        return pl.ds(pl.multiple_of(r * 3072 + k * CHUNK, 128), CHUNK)

    half = pl.ds(pl.multiple_of(x_hi * 64, 64), 64)

    def send_x(a):
        i = POS[1, (-a) % 4]
        r = (1 - x_lo) * 4 + (y + a + 4) % 4
        for pp in range(2 if a == 0 else 1):
            p = (par + pp) % 2
            for t in range(2):
                k = chunk_of(p, t, core)
                for n, step in enumerate((1, -1)):
                    send(hidden.at[half, cols(r, k)], hid.at[k, i, half, :], hx_s.at[pp, t, i, n],
                         hx_r.at[pp, t, i, x_hi], dev(step, a, 0, 0))

    def send_y(t):
        k = chunk_of(par, t, core)
        for n, a in enumerate((1, -1, 2)):
            i = POS[0, (-a) % 4]
            r = x_lo * 4 + (y + a + 4) % 4
            send(hidden.at[:, cols(r, k)], hid.at[k, i], hy_s.at[t, n], hy_r.at[t, i], dev(0, a, 0, 0))

    send_x(0)
    i = POS[1, 0]
    arrived(og_all.at[i], g_r.at[i])
    for n, a in enumerate((1, -1, 2)):
        j = POS[1, (-a) % 4]
        send(og_all.at[i], og_all.at[j], g_s.at[4 + n], g_r.at[j], dev(0, a, 0, 0))

    def compute_pair(pair):
        ia, ib = 2 * pair, 2 * pair + 1
        f_copies[ia].wait()
        f_copies[ib].wait()
        rows = [pl.multiple_of(row_of(SLOTS[i]) * 128, 128) for i in (ia, ib)]

        def one(b, _):
            units = pl.ds(pl.multiple_of(b * 512, 512), 512)
            codes = pl.ds(pl.multiple_of(b * 128, 128), 128)
            grads = og_all[ia:ib + 1].reshape(256, 384)
            part = dot(grads, w_buf[units, :], NT)
            acc = part + fbuf[ia:ib + 1, :, units].reshape(256, 512).astype(F32)
            code = dot(acc.astype(BF16), comp_ref[...], NN)
            cbuf[ia:ib + 1, :, codes] = code.reshape(2, 128, 128)
            fresh = (acc - dot(code.astype(BF16), comp_ref[...], NT)).astype(BF16)
            nf_ref[0, pl.ds(rows[0], 128), units] = fresh[:128]
            nf_ref[0, pl.ds(rows[1], 128), units] = fresh[128:]
            return 0

        lax.fori_loop(0, 6, one, 0)
        theirs = pl.ds(pl.multiple_of((1 - core) * 64, 64), 64)
        for i in (ia, ib):
            send(cbuf.at[i, theirs, :], pbuf.at[i], p_s.at[i], p_r.at[i], dev(0, 0, 0, 1))

    def reduce_pair(pair):
        mine = pl.ds(pl.multiple_of(core * 64, 64), 64)
        for i in (2 * pair, 2 * pair + 1):
            dx, dy = SLOTS[i]
            arrived(pbuf.at[i], p_r.at[i])
            xl = x_lo if dx == 0 else 1 - x_lo

            @pl.when(xl == x_hi)
            def _():
                ksum[dy] = cbuf[i, mine, :] + pbuf[i]

            @pl.when(xl != x_hi)
            def _():
                csend[dy] = (cbuf[i, mine, :] + pbuf[i]).astype(BF16)
                pltpu.make_async_remote_copy(
                    src_ref=csend.at[dy], dst_ref=cx.at[dy], send_sem=cx_s.at[dy], recv_sem=cx_r.at[dy],
                    device_id=dev(2, 0, 0, 0), device_id_type=MESH).start()

    w_copy.wait()
    compute_pair(0)
    for i in (2, 3):
        arrived(og_all.at[i], g_r.at[i])
    compute_pair(1)
    send_y(0)
    send_y(1)
    reduce_pair(0)
    for i in (4, 5):
        arrived(og_all.at[i], g_r.at[i])
    compute_pair(2)
    send_x(1)
    send_x(-1)
    send_x(2)
    reduce_pair(1)
    for i in (6, 7):
        arrived(og_all.at[i], g_r.at[i])
    compute_pair(3)
    reduce_pair(2)

    mine_k = [chunk_of(par, t, core) for t in range(2)]
    near_k = [chunk_of(1 - par, t, core) for t in range(2)]

    def pass_z(t, i):
        k = mine_k[t]
        send(hid.at[k, i], hid.at[k, i], hz_s.at[t, i], hz_r.at[t, i], dev(0, 0, z_steps[t], 0))

    for t in range(2):
        for i in (2, 3, 4):
            arrived(hid.at[mine_k[t], i], hy_r.at[t, i])
            pass_z(t, i)

    for i in range(8):
        og_t[:, i * 128:(i + 1) * 128] = og_all[i].T

    reduce_pair(3)

    for dy in range(4):
        arrived(cx.at[dy], cx_r.at[dy])
        to = (y + dy) % 4

        @pl.when(to == z)
        def _():
            tot[...] = ksum[dy] + cx[dy].astype(F32)

        @pl.when(to != z)
        def _():
            cs2[dy] = (ksum[dy] + cx[dy].astype(F32)).astype(BF16)
            slot = (z - to + 4) % 4 - 1
            pltpu.make_async_remote_copy(
                src_ref=cs2.at[dy], dst_ref=cz.at[slot], send_sem=cz_s.at[dy], recv_sem=cz_r.at[slot],
                device_id=dev(0, 0, to - z, 0), device_id_type=MESH).start()

    for i in (5, 6, 7):
        for t in range(2):
            for q in range(2):
                arrived(hid.at[mine_k[t], i, q * 64:(q + 1) * 64, :], hx_r.at[0, t, i, q])
            pass_z(t, i)
    for pp in range(2):
        for t in range(2):
            k = chunk_of((par + pp) % 2, t, core)
            for q in range(2):
                arrived(hid.at[k, 1, q * 64:(q + 1) * 64, :], hx_r.at[pp, t, 1, q])

    def pass_core(pp, t):
        k = chunk_of((par + pp) % 2, t, core)
        send(hid.at[k, 1:8], hid.at[k, 1:8], hc_s.at[pp, t], hc_r.at[pp, t], dev(0, 0, 0, 1))

    def weight_grad(k):
        out = dot(og_t[...], hid[k].reshape(1024, CHUNK), NN)
        gw_ref[pl.ds(pl.multiple_of(k * CHUNK, CHUNK), CHUNK), :] = out.T.astype(BF16)

    for t in range(2):
        pass_core(0, t)
    for cp in own_copies:
        cp.wait()
    for t in range(2):
        weight_grad(mine_k[t])
    for t in range(2):
        k = chunk_of(par, t, 1 - core)
        arrived(hid.at[k, 1:8], hc_r.at[0, t])
        weight_grad(k)

    for slot in range(3):
        arrived(cz.at[slot], cz_r.at[slot])
    total = tot[...] + cz[0].astype(F32) + cz[1].astype(F32) + cz[2].astype(F32)
    low = total.astype(BF16)
    for b in range(6):
        gi_ref[:, b * 512:(b + 1) * 512] = dot(low[:, b * 128:(b + 1) * 128], comp_ref[...], NT).astype(BF16)

    for t in range(2):
        for i in range(2, 8):
            arrived(hid.at[near_k[t], i], hz_r.at[t, i])
        pass_core(1, t)
    for t in range(2):
        weight_grad(near_k[t])
    for t in range(2):
        k = chunk_of(1 - par, t, 1 - core)
        arrived(hid.at[k, 1:8], hc_r.at[1, t])
        weight_grad(k)

    for cp in sends:
        cp.wait_send()
    for dy in range(4):
        pltpu.make_async_copy(csend.at[dy], csend.at[dy], cx_s.at[dy]).wait()

        @pl.when((y + dy) % 4 != z)
        def _():
            pltpu.make_async_copy(cs2.at[dy], cs2.at[dy], cz_s.at[dy]).wait()


def on_device(out_grad, hidden, weight, compress, feedback):
    dma = pltpu.SemaphoreType.DMA
    vmem = pl.BlockSpec(memory_space=pltpu.VMEM)
    hbm = pl.BlockSpec(memory_space=pl.ANY)
    return pl.pallas_call(
        body,
        out_shape=(
            OUT((64, 3072), BF16),
            OUT((3072, 384), BF16),
            OUT((1, 1024, 3072), BF16),
        ),
        in_specs=[vmem, hbm, hbm, vmem, hbm],
        out_specs=(vmem, vmem, vmem),
        scratch_shapes=[
            pltpu.VMEM((8, 128, 384), BF16),
            pltpu.VMEM((384, 1024), BF16),
            pltpu.VMEM((3072, 384), BF16),
            pltpu.VMEM((8, 128, 3072), BF16),
            pltpu.VMEM((8, 8, 128, CHUNK), BF16),
            pltpu.VMEM((8, 128, 768), F32),
            pltpu.VMEM((8, 64, 768), F32),
            pltpu.VMEM((4, 64, 768), BF16),
            pltpu.VMEM((4, 64, 768), BF16),
            pltpu.VMEM((4, 64, 768), F32),
            pltpu.VMEM((4, 64, 768), BF16),
            pltpu.VMEM((3, 64, 768), BF16),
            pltpu.VMEM((64, 768), F32),
            dma((7,)), dma((8,)), dma((2, 3)), dma((2, 8)),
            dma((2, 2, 8, 2)), dma((2, 2, 8, 2)), dma((2, 8)), dma((2, 8)),
            dma((2, 2)), dma((2, 2)),
            dma((8,)), dma((8,)), dma((4,)), dma((4,)), dma((4,)), dma((3,)),
            dma, dma((8,)), dma((8,)),
        ],
        compiler_params=pltpu.CompilerParams(
            collective_id=0, has_side_effects=True, vmem_limit_bytes=48 * 2**20
        ),
        cost_estimate=pl.CostEstimate(flops=6_500_000_000, bytes_accessed=25_000_000, transcendentals=0),
    )(out_grad, hidden, weight, compress, feedback)


OUT = jax.ShapeDtypeStruct


def solution(mesh):
    return jax.shard_map(
        on_device,
        mesh=mesh,
        in_specs=(P("row", "col"), P("row", None), P("row", "col"), P(), P("col", None, "row")),
        out_specs=(P("col", "row"), P("row", "col"), P("col", None, "row")),
        check_vma=False,
    )
```

```python
import jax
import jax.numpy as jnp
from jax import lax
from jax.experimental import pallas as pl
from jax.experimental.pallas import tpu as pltpu
from jax.sharding import PartitionSpec as P

MESH = pl.DeviceIdType.MESH
NT = (((1,), (1,)), ((), ()))
NN = (((1,), (0,)), ((), ()))
F32 = jnp.float32
BF16 = jnp.bfloat16

SLOTS = [(0, 0), (1, 0), (0, 1), (0, 3), (0, 2), (1, 1), (1, 3), (1, 2)]
POS = {slot: i for i, slot in enumerate(SLOTS)}
CHUNK = 384


def dot(a, b, dims):
    return lax.dot_general(a, b, dims, preferred_element_type=F32)


def body(og_ref, hidden, weight, compress, feedback, gi_ref, gw_ref, nf_ref,
         og_all, og_t, comp_ref, rel, w_buf, fbuf, hid, cbuf, pbuf, csend, cx, ksum, cs2, cz, tot,
         g_s, g_r, hy_s, hy_r, rl_s, rl_r, xo_s, xo_r, hx_s, hx_r, hz_s, hz_r, hc_s, hc_r,
         p_s, p_r, cx_s, cx_r, cz_s, cz_r, comp_sem, og_sem, w_sem, f_sem, own_sem):
    row = lax.axis_index("row")
    col = lax.axis_index("col")
    x_lo, y = row // 4, row % 4
    core, z, x_hi = col % 2, (col // 2) % 4, col // 8
    x = x_hi * 2 + x_lo

    def dev(dx, dy, dz, dc):
        xx, yy, zz, cc = (x + dx + 4) % 4, (y + dy + 4) % 4, (z + dz + 4) % 4, (core + dc) % 2
        return ((xx % 2) * 4 + yy, ((xx // 2) * 4 + zz) * 2 + cc)

    x_pair = 1 - 2 * x_lo
    par = z % 2

    def z_step(t):
        return (1 - 2 * ((t + core) % 2)) * (1 - 2 * par)

    barrier = pltpu.get_barrier_semaphore()
    peers = [dev(0, 1, 0, 0), dev(0, -1, 0, 0), dev(0, 2, 0, 0), dev(1, 0, 0, 0), dev(-1, 0, 0, 0), dev(2, 0, 0, 0),
             dev(0, 0, 1, 0), dev(0, 0, -1, 0), dev(0, 0, 2, 0), dev(0, 0, 0, 1)]
    for peer in peers:
        pl.semaphore_signal(barrier, inc=1, device_id=peer, device_id_type=MESH)

    def row_of(slot):
        dx, dy = slot
        xl = x_lo if dx == 0 else 1 - x_lo
        return xl * 4 + (y + dy) % 4

    comp_copy = pltpu.make_async_copy(compress, comp_ref, comp_sem)
    comp_copy.start()
    og_copy = pltpu.make_async_copy(og_ref, og_all.at[0], og_sem)
    og_copy.start()
    w_copy = pltpu.make_async_copy(weight, w_buf, w_sem)
    w_copy.start()
    f_copies = []
    for i, slot in enumerate(SLOTS):
        start = pl.multiple_of(row_of(slot) * 128, 128)
        cp = pltpu.make_async_copy(feedback.at[0, pl.ds(start, 128), :], fbuf.at[i], f_sem.at[i])
        cp.start()
        f_copies.append(cp)
    own_copies = []
    for k in range(8):
        start = pl.multiple_of(row * 3072 + k * CHUNK, 128)
        cp = pltpu.make_async_copy(hidden.at[:, pl.ds(start, CHUNK)], hid.at[k, 0], own_sem.at[k])
        cp.start()
        own_copies.append(cp)

    pl.semaphore_wait(barrier, len(peers))

    sends = []

    def send(src, dst, s_sem, r_sem, to):
        cp = pltpu.make_async_remote_copy(src_ref=src, dst_ref=dst, send_sem=s_sem, recv_sem=r_sem,
                                          device_id=to, device_id_type=MESH)
        cp.start()
        sends.append(cp)
        return cp

    def arrived(dst, sem):
        pltpu.make_async_copy(dst, dst, sem).wait()

    def send_grads():
        og_copy.wait()
        i = POS[1, 0]
        send(og_all.at[0], og_all.at[i], g_s.at[0], g_r.at[i], dev(x_pair, 0, 0, 0))
        for n, a in enumerate((1, -1, 2)):
            i = POS[0, (-a) % 4]
            send(og_all.at[0], og_all.at[i], g_s.at[1 + n], g_r.at[i], dev(0, a, 0, 0))

    def chunk_of(p, t, c):
        return p * 4 + t * 2 + c

    def cols(r, k):
        return pl.ds(pl.multiple_of(r * 3072 + k * CHUNK, 128), CHUNK)

    half = pl.ds(pl.multiple_of(x_hi * 64, 64), 64)

    def send_x_only(t):
        for pp in range(2):
            k = chunk_of((par + pp) % 2, t, core)
            for n, step in enumerate((1, -1)):
                send(hidden.at[half, cols((1 - x_lo) * 4 + y, k)], hid.at[k, 1, half, :], xo_s.at[pp, t, n],
                     xo_r.at[pp, t, x_hi], dev(step, 0, 0, 0))

    def send_relay(t, a):
        k = chunk_of(par, t, core)
        d = (-a) % 4 - 1
        send(hidden.at[half, cols((1 - x_lo) * 4 + (y + a + 4) % 4, k)], rel.at[t, d], rl_s.at[t, d], rl_r.at[t, d],
             dev(0, a, 0, 0))

    def send_y(t, a):
        k = chunk_of(par, t, core)
        i = POS[0, (-a) % 4]
        send(hidden.at[:, cols(x_lo * 4 + (y + a + 4) % 4, k)], hid.at[k, i], hy_s.at[t, i], hy_r.at[t, i],
             dev(0, a, 0, 0))

    def pass_x(t, d):
        k = chunk_of(par, t, core)
        arrived(rel.at[t, d], rl_r.at[t, d])
        for n, step in enumerate((1, -1)):
            send(rel.at[t, d], hid.at[k, POS[1, d + 1], half, :], hx_s.at[t, d, n], hx_r.at[t, d, x_hi],
                 dev(step, 0, 0, 0))

    def send_grads_on():
        i = POS[1, 0]
        arrived(og_all.at[i], g_r.at[i])
        for n, a in enumerate((1, -1, 2)):
            j = POS[1, (-a) % 4]
            send(og_all.at[i], og_all.at[j], g_s.at[4 + n], g_r.at[j], dev(0, a, 0, 0))

    def compute_half(pair, h):
        ia, ib = 2 * pair, 2 * pair + 1
        if h == 0:
            f_copies[ia].wait()
            f_copies[ib].wait()
        rows = [pl.multiple_of(row_of(SLOTS[i]) * 128, 128) for i in (ia, ib)]

        def one(b, _):
            units = pl.ds(pl.multiple_of(b * 512, 512), 512)
            codes = pl.ds(pl.multiple_of(b * 128, 128), 128)
            grads = og_all[ia:ib + 1].reshape(256, 384)
            part = dot(grads, w_buf[units, :], NT)
            acc = part + fbuf[ia:ib + 1, :, units].reshape(256, 512).astype(F32)
            code = dot(acc.astype(BF16), comp_ref[...], NN)
            cbuf[ia:ib + 1, :, codes] = code.reshape(2, 128, 128)
            fresh = (acc - dot(code.astype(BF16), comp_ref[...], NT)).astype(BF16)
            nf_ref[0, pl.ds(rows[0], 128), units] = fresh[:128]
            nf_ref[0, pl.ds(rows[1], 128), units] = fresh[128:]
            return 0

        lax.fori_loop(3 * h, 3 * h + 3, one, 0, unroll=True)
        if h == 0:
            return
        theirs = pl.ds(pl.multiple_of((1 - core) * 64, 64), 64)
        for i in (ia, ib):
            send(cbuf.at[i, theirs, :], pbuf.at[i], p_s.at[i], p_r.at[i], dev(0, 0, 0, 1))

    def reduce_slot(i):
        mine = pl.ds(pl.multiple_of(core * 64, 64), 64)
        dx, dy = SLOTS[i]
        arrived(pbuf.at[i], p_r.at[i])
        xl = x_lo if dx == 0 else 1 - x_lo

        @pl.when(xl == x_hi)
        def _():
            ksum[dy] = cbuf[i, mine, :] + pbuf[i]

        @pl.when(xl != x_hi)
        def _():
            csend[dy] = (cbuf[i, mine, :] + pbuf[i]).astype(BF16)
            pltpu.make_async_remote_copy(
                src_ref=csend.at[dy], dst_ref=cx.at[dy], send_sem=cx_s.at[dy], recv_sem=cx_r.at[dy],
                device_id=dev(2, 0, 0, 0), device_id_type=MESH).start()

    def gather(*slots):
        for i in slots:
            arrived(og_all.at[i], g_r.at[i])

    def mine_k(t):
        return chunk_of(par, t, core)

    def near_k(t):
        return chunk_of(1 - par, t, core)

    def pass_z(t, i):
        k = mine_k(t)
        send(hid.at[k, i], hid.at[k, i], hz_s.at[t, i], hz_r.at[t, i], dev(0, 0, z_step(t), 0))

    def own_z(t, *dys):
        for dy in dys:
            i = POS[0, dy]
            arrived(hid.at[mine_k(t), i], hy_r.at[t, i])
            pass_z(t, i)

    def other_z(t, *ds):
        for d in ds:
            i = POS[1, d + 1]
            for q in range(2):
                arrived(hid.at[mine_k(t), i, q * 64:(q + 1) * 64, :], hx_r.at[t, d, q])
            pass_z(t, i)

    def x_only(pp, t):
        k = chunk_of((par + pp) % 2, t, core)
        for q in range(2):
            arrived(hid.at[k, 1, q * 64:(q + 1) * 64, :], xo_r.at[pp, t, q])

    groups = (pl.ds(5, 3), pl.ds(1, 4))

    def pass_core(pp, t, g):
        part = hid.at[chunk_of((par + pp) % 2, t, core), groups[g]]
        send(part, part, hc_s.at[pp, t, g], hc_r.at[pp, t, g], dev(0, 0, 0, 1))

    def near_z(t, *slots):
        for i in slots:
            arrived(hid.at[near_k(t), i], hz_r.at[t, i])

    def weight_grad(k):
        out = dot(og_t[...], hid[k].reshape(1024, CHUNK), NN)
        gw_ref[pl.ds(pl.multiple_of(k * CHUNK, CHUNK), CHUNK), :] = out.T.astype(BF16)

    def partner_grad(pp, t):
        k = chunk_of((par + pp) % 2, t, 1 - core)
        for g in range(2):
            arrived(hid.at[k, groups[g]], hc_r.at[pp, t, g])
        weight_grad(k)

    def codes_z(e):
        dy = (z + e - y + 4) % 4
        arrived(cx.at[dy], cx_r.at[dy])
        part = ksum[dy] + cx[dy].astype(F32)
        if e == 0:
            tot[...] = part
        else:
            cs2[e - 1] = part.astype(BF16)
            send(cs2.at[e - 1], cz.at[3 - e], cz_s.at[e - 1], cz_r.at[3 - e], dev(0, 0, e, 0))


    def input_grad():
        for slot in range(3):
            arrived(cz.at[slot], cz_r.at[slot])
        total = tot[...] + cz[0].astype(F32) + cz[1].astype(F32) + cz[2].astype(F32)
        low = total.astype(BF16)
        for b in range(6):
            gi_ref[:, b * 512:(b + 1) * 512] = dot(low[:, b * 128:(b + 1) * 128], comp_ref[...], NT).astype(BF16)

    def transpose_grads():
        for i in range(8):
            og_t[:, i * 128:(i + 1) * 128] = og_all[i].T

    send_grads()
    send_relay(1, -1)
    send_x_only(1)
    send_relay(0, 1)
    send_relay(0, -1)
    send_x_only(0)
    send_relay(1, 1)
    send_grads_on()
    comp_copy.wait()
    w_copy.wait()
    compute_half(0, 0)
    gather(3)
    gather(2)
    send_relay(1, 2)
    send_y(1, -1)
    compute_half(1, 0)
    send_y(0, 1)
    send_relay(0, 2)
    send_y(0, -1)
    send_y(1, 1)
    x_only(0, 1)
    pass_x(0, 2)
    pass_x(1, 0)
    gather(4)
    x_only(0, 0)
    compute_half(0, 1)
    pass_x(0, 0)
    pass_x(1, 2)
    compute_half(1, 1)
    send_y(1, 2)
    reduce_slot(1)
    other_z(0, 2)
    gather(5)
    compute_half(2, 0)
    other_z(1, 0)
    gather(6)
    reduce_slot(2)
    compute_half(2, 1)
    gather(7)
    other_z(1, 2)
    other_z(0, 0)
    pass_x(1, 1)
    reduce_slot(0)
    compute_half(3, 0)
    reduce_slot(5)
    own_z(1, 1)
    compute_half(3, 1)
    own_z(0, 3)
    send_y(0, 2)
    pass_x(0, 1)
    reduce_slot(4)
    x_only(1, 1)
    reduce_slot(3)
    other_z(1, 1)
    pass_core(0, 1, 0)
    reduce_slot(6)
    own_z(0, 1)
    own_z(1, 3)
    reduce_slot(7)
    own_z(1, 2)
    pass_core(0, 1, 1)
    other_z(0, 1)
    transpose_grads()
    near_z(1, 5)
    for cp in own_copies:
        cp.wait()
    weight_grad(mine_k(1))
    near_z(1, 6)
    near_z(1, 2)
    near_z(1, 7)
    near_z(0, 6)
    near_z(0, 2)
    own_z(0, 2)
    codes_z(2)
    partner_grad(0, 1)
    near_z(0, 3)
    pass_core(0, 0, 0)
    codes_z(1)
    codes_z(3)
    pass_core(0, 0, 1)
    pass_core(1, 1, 0)
    near_z(0, 5)
    codes_z(0)
    weight_grad(mine_k(0))
    near_z(0, 4)
    near_z(1, 4)
    near_z(0, 7)
    x_only(1, 0)
    pass_core(1, 0, 0)
    near_z(1, 3)
    pass_core(1, 0, 1)
    pass_core(1, 1, 1)
    partner_grad(0, 0)
    weight_grad(near_k(0))
    partner_grad(1, 0)
    weight_grad(near_k(1))
    partner_grad(1, 1)
    input_grad()

    for cp in sends:
        cp.wait_send()
    for dy in range(4):
        pltpu.make_async_copy(csend.at[dy], csend.at[dy], cx_s.at[dy]).wait()


def on_device(out_grad, hidden, weight, compress, feedback):
    dma = pltpu.SemaphoreType.DMA
    vmem = pl.BlockSpec(memory_space=pltpu.VMEM)
    hbm = pl.BlockSpec(memory_space=pltpu.HBM)
    return pl.pallas_call(
        body,
        out_shape=(
            OUT((64, 3072), BF16),
            OUT((3072, 384), BF16),
            OUT((1, 1024, 3072), BF16),
        ),
        in_specs=[hbm] * 5,
        out_specs=(vmem, vmem, vmem),
        scratch_shapes=[
            pltpu.VMEM((8, 128, 384), BF16),
            pltpu.VMEM((384, 1024), BF16),
            pltpu.VMEM((512, 128), BF16),
            pltpu.VMEM((2, 3, 64, CHUNK), BF16),
            pltpu.VMEM((3072, 384), BF16),
            pltpu.VMEM((8, 128, 3072), BF16),
            pltpu.VMEM((8, 8, 128, CHUNK), BF16),
            pltpu.VMEM((8, 128, 768), F32),
            pltpu.VMEM((8, 64, 768), F32),
            pltpu.VMEM((4, 64, 768), BF16),
            pltpu.VMEM((4, 64, 768), BF16),
            pltpu.VMEM((4, 64, 768), F32),
            pltpu.VMEM((3, 64, 768), BF16),
            pltpu.VMEM((3, 64, 768), BF16),
            pltpu.VMEM((64, 768), F32),
            dma((7,)), dma((8,)), dma((2, 8)), dma((2, 8)), dma((2, 3)), dma((2, 3)),
            dma((2, 2, 2)), dma((2, 2, 2)), dma((2, 3, 2)), dma((2, 3, 2)), dma((2, 8)), dma((2, 8)),
            dma((2, 2, 2)), dma((2, 2, 2)),
            dma((8,)), dma((8,)), dma((4,)), dma((4,)), dma((3,)), dma((3,)),
            dma, dma, dma, dma((8,)), dma((8,)),
        ],
        compiler_params=pltpu.CompilerParams(
            collective_id=0, has_side_effects=True, vmem_limit_bytes=36 * 2**20
        ),
        cost_estimate=pl.CostEstimate(flops=6_500_000_000, bytes_accessed=25_000_000, transcendentals=0),
    )(*[pltpu.with_memory_space_constraint(a, pltpu.HBM) for a in (out_grad, hidden, weight, compress, feedback)])


OUT = pltpu.VMEM


def solution(mesh):
    return jax.shard_map(
        on_device,
        mesh=mesh,
        in_specs=(P("row", "col"), P("row", None), P("row", "col"), P(), P("col", None, "row")),
        out_specs=(P("col", "row"), P("row", "col"), P("col", None, "row")),
        check_vma=False,
    )
```

```python
import jax
import jax.numpy as jnp
from jax import lax
from jax.experimental import pallas as pl
from jax.experimental.pallas import tpu as pltpu
from jax.sharding import PartitionSpec as P

MESH = pl.DeviceIdType.MESH
NT = (((1,), (1,)), ((), ()))
NN = (((1,), (0,)), ((), ()))
F32 = jnp.float32
BF16 = jnp.bfloat16

SLOTS = [(0, 0), (1, 0), (0, 1), (0, 3), (0, 2), (1, 1), (1, 3), (1, 2)]
POS = {slot: i for i, slot in enumerate(SLOTS)}
CHUNK = 384
DIRECT = ((0, 1), (0, 3), (1, 1), (1, 3))


def dot(a, b, dims):
    return lax.dot_general(a, b, dims, preferred_element_type=F32)


def body(og_ref, hidden, weight, compress, feedback, gi_ref, gw_ref, nf_ref,
         og_all, og_t, comp_ref, rel, w_buf, fbuf, hid, cbuf, pbuf, csend, cx, ksum, cs2, cz, tot,
         g_s, g_r, gf_s, gf_r, hy_s, hy_r, rl_s, rl_r, xo_s, xo_r, hx_s, hx_r, hz_s, hz_r, hc_s, hc_r,
         p_s, p_r, cx_s, cx_r, cz_s, cz_r, comp_sem, og_sem, w_sem, f_sem, own_sem):
    row = lax.axis_index("row")
    col = lax.axis_index("col")
    x_lo, y = row // 4, row % 4
    core, z, x_hi = col % 2, (col // 2) % 4, col // 8
    x = x_hi * 2 + x_lo

    def dev(dx, dy, dz, dc):
        xx, yy, zz, cc = (x + dx + 4) % 4, (y + dy + 4) % 4, (z + dz + 4) % 4, (core + dc) % 2
        return ((xx % 2) * 4 + yy, ((xx // 2) * 4 + zz) * 2 + cc)

    x_pair = 1 - 2 * x_lo
    par = z % 2

    def z_step(t):
        return (1 - 2 * ((t + core) % 2)) * (1 - 2 * par)

    barrier = pltpu.get_barrier_semaphore()
    peers = [dev(0, 1, 0, 0), dev(0, -1, 0, 0), dev(0, 2, 0, 0), dev(1, 0, 0, 0), dev(-1, 0, 0, 0), dev(2, 0, 0, 0),
             dev(0, 0, 1, 0), dev(0, 0, -1, 0), dev(0, 0, 2, 0), dev(0, 0, 0, 1)]
    for peer in peers:
        pl.semaphore_signal(barrier, inc=1, device_id=peer, device_id_type=MESH)

    def row_of(slot):
        dx, dy = slot
        xl = x_lo if dx == 0 else 1 - x_lo
        return xl * 4 + (y + dy) % 4

    comp_copy = pltpu.make_async_copy(compress, comp_ref, comp_sem)
    comp_copy.start()
    og_copy = pltpu.make_async_copy(og_ref, og_all.at[0], og_sem)
    og_copy.start()
    w_copy = pltpu.make_async_copy(weight, w_buf, w_sem)
    w_copy.start()
    f_copies = []
    for i, slot in enumerate(SLOTS):
        start = pl.multiple_of(row_of(slot) * 128, 128)
        cp = pltpu.make_async_copy(feedback.at[0, pl.ds(start, 128), :], fbuf.at[i], f_sem.at[i])
        cp.start()
        f_copies.append(cp)
    own_copies = []
    for k in range(8):
        start = pl.multiple_of(row * 3072 + k * CHUNK, 128)
        cp = pltpu.make_async_copy(hidden.at[:, pl.ds(start, CHUNK)], hid.at[k, 0], own_sem.at[k])
        cp.start()
        own_copies.append(cp)

    pl.semaphore_wait(barrier, len(peers))

    sends = []

    def send(src, dst, s_sem, r_sem, to):
        cp = pltpu.make_async_remote_copy(src_ref=src, dst_ref=dst, send_sem=s_sem, recv_sem=r_sem,
                                          device_id=to, device_id_type=MESH)
        cp.start()
        sends.append(cp)
        return cp

    def arrived(dst, sem):
        pltpu.make_async_copy(dst, dst, sem).wait()

    def send_grads():
        og_copy.wait()
        i = POS[1, 0]
        send(og_all.at[0], og_all.at[i], g_s.at[0], g_r.at[i], dev(x_pair, 0, 0, 0))
        for n, a in enumerate((1, -1)):
            i = POS[0, (-a) % 4]
            send(og_all.at[0], og_all.at[i], g_s.at[1 + n], g_r.at[i], dev(0, a, 0, 0))

    def chunk_of(p, t, c):
        return p * 4 + t * 2 + c

    def cols(r, k):
        return pl.ds(pl.multiple_of(r * 3072 + k * CHUNK, 128), CHUNK)

    half = pl.ds(pl.multiple_of(x_hi * 64, 64), 64)

    def send_x_only(t):
        for pp in range(2):
            k = chunk_of((par + pp) % 2, t, core)
            for n, step in enumerate((1, -1)):
                send(hidden.at[half, cols((1 - x_lo) * 4 + y, k)], hid.at[k, 1, half, :], xo_s.at[pp, t, n],
                     xo_r.at[pp, t, x_hi], dev(step, 0, 0, 0))

    def send_relay(t, a):
        k = chunk_of(par, t, core)
        d = (-a) % 4 - 1
        send(hidden.at[half, cols((1 - x_lo) * 4 + (y + a + 4) % 4, k)], rel.at[t, d], rl_s.at[t, d], rl_r.at[t, d],
             dev(0, a, 0, 0))

    def send_y(t, a):
        k = chunk_of(par, t, core)
        i = POS[0, (-a) % 4]
        send(hidden.at[:, cols(x_lo * 4 + (y + a + 4) % 4, k)], hid.at[k, i], hy_s.at[t, i], hy_r.at[t, i],
             dev(0, a, 0, 0))
        if (t, (-a) % 4) in DIRECT:
            k = chunk_of(1 - par, t, core)
            send(hidden.at[:, cols(x_lo * 4 + (y + a + 4) % 4, k)], hid.at[k, i], hz_s.at[t, i], hz_r.at[t, i],
                 dev(0, a, 0, 0))

    def pass_x(t, d):
        k = chunk_of(par, t, core)
        arrived(rel.at[t, d], rl_r.at[t, d])
        for n, step in enumerate((1, -1)):
            send(rel.at[t, d], hid.at[k, POS[1, d + 1], half, :], hx_s.at[t, d, n], hx_r.at[t, d, x_hi],
                 dev(step, 0, 0, 0))

    def send_grads_on():
        i = POS[1, 0]
        arrived(og_all.at[i], g_r.at[i])
        for n, a in enumerate((1, -1)):
            j = POS[1, (-a) % 4]
            send(og_all.at[i], og_all.at[j], g_s.at[4 + n], g_r.at[j], dev(0, a, 0, 0))

    def compute_half(pair, h):
        ia, ib = (2 * pair, 2 * pair + 1) if pair else (h, h)
        if h == 0 or pair == 0:
            f_copies[ia].wait()
        if h == 0 and pair > 0:
            f_copies[ib].wait()
        rows = [pl.multiple_of(row_of(SLOTS[i]) * 128, 128) for i in range(ia, ib + 1)]
        n = ib + 1 - ia

        blocks = range(3 * h, 3 * h + 3) if pair else range(6)
        grads = og_all[ia:ib + 1].reshape(n * 128, 384)
        accs = []
        for b in blocks:
            u = slice(b * 512, b * 512 + 512)
            accs.append(dot(grads, w_buf[u, :], NT) + fbuf[ia:ib + 1, :, u].reshape(n * 128, 512).astype(F32))
        lows = []
        for b, acc in zip(blocks, accs):
            code = dot(acc.astype(BF16), comp_ref[...], NN)
            cbuf[ia:ib + 1, :, b * 128:b * 128 + 128] = code.reshape(n, 128, 128)
            lows.append(code.astype(BF16))
        for b, acc, low in zip(blocks, accs, lows):
            u = slice(b * 512, b * 512 + 512)
            fresh = (acc - dot(low, comp_ref[...], NT)).astype(BF16)
            for j in range(n):
                nf_ref[0, pl.ds(rows[j], 128), u] = fresh[j * 128:j * 128 + 128]
        if h == 0 and pair > 0:
            return
        theirs = pl.ds(pl.multiple_of((1 - core) * 64, 64), 64)
        for i in range(ia, ib + 1):
            send(cbuf.at[i, theirs, :], pbuf.at[i], p_s.at[i], p_r.at[i], dev(0, 0, 0, 1))

    def reduce_slot(i):
        mine = pl.ds(pl.multiple_of(core * 64, 64), 64)
        dx, dy = SLOTS[i]
        arrived(pbuf.at[i], p_r.at[i])
        xl = x_lo if dx == 0 else 1 - x_lo

        @pl.when(xl == x_hi)
        def _():
            ksum[dy] = cbuf[i, mine, :] + pbuf[i]

        @pl.when(xl != x_hi)
        def _():
            csend[dy] = (cbuf[i, mine, :] + pbuf[i]).astype(BF16)
            pltpu.make_async_remote_copy(
                src_ref=csend.at[dy], dst_ref=cx.at[dy], send_sem=cx_s.at[dy], recv_sem=cx_r.at[dy],
                device_id=dev(2, 0, 0, 0), device_id_type=MESH).start()

    halves = (pl.ds(0, 64), pl.ds(64, 64))

    def gather(i):
        dx, dy = SLOTS[i]
        if dy == 2:
            for h in range(2):
                arrived(og_all.at[i, halves[h], :], gf_r.at[dx, h])
        else:
            arrived(og_all.at[i], g_r.at[i])

    def pass_grads(dx, h):
        i, j = POS[dx, 1 + 2 * h], POS[dx, 2]
        send(og_all.at[i, halves[h], :], og_all.at[j, halves[h], :], gf_s.at[dx, h], gf_r.at[dx, h],
             dev(0, 2 * h - 1, 0, 0))

    def mine_k(t):
        return chunk_of(par, t, core)

    def near_k(t):
        return chunk_of(1 - par, t, core)

    def pass_z(t, i):
        k = mine_k(t)
        send(hid.at[k, i], hid.at[k, i], hz_s.at[t, i], hz_r.at[t, i], dev(0, 0, z_step(t), 0))

    def own_z(t, *dys):
        for dy in dys:
            i = POS[0, dy]
            arrived(hid.at[mine_k(t), i], hy_r.at[t, i])
            if (t, dy) not in DIRECT:
                pass_z(t, i)

    def other_z(t, *ds):
        for d in ds:
            i = POS[1, d + 1]
            for q in range(2):
                arrived(hid.at[mine_k(t), i, q * 64:(q + 1) * 64, :], hx_r.at[t, d, q])
            pass_z(t, i)

    def x_only(pp, t):
        k = chunk_of((par + pp) % 2, t, core)
        for q in range(2):
            arrived(hid.at[k, 1, q * 64:(q + 1) * 64, :], xo_r.at[pp, t, q])

    groups = (pl.ds(5, 3), pl.ds(1, 4))

    def pass_core(pp, t, g):
        part = hid.at[chunk_of((par + pp) % 2, t, core), groups[g]]
        send(part, part, hc_s.at[pp, t, g], hc_r.at[pp, t, g], dev(0, 0, 0, 1))

    def near_z(t, *slots):
        for i in slots:
            arrived(hid.at[near_k(t), i], hz_r.at[t, i])

    def weight_grad(k):
        out = dot(og_t[...], hid[k].reshape(1024, CHUNK), NN)
        gw_ref[pl.ds(pl.multiple_of(k * CHUNK, CHUNK), CHUNK), :] = out.T.astype(BF16)

    def partner_grad(pp, t):
        k = chunk_of((par + pp) % 2, t, 1 - core)
        for g in range(2):
            arrived(hid.at[k, groups[g]], hc_r.at[pp, t, g])
        weight_grad(k)

    def codes_z(e):
        dy = (z + e - y + 4) % 4
        arrived(cx.at[dy], cx_r.at[dy])
        part = ksum[dy] + cx[dy].astype(F32)
        if e == 0:
            tot[...] = part
        else:
            cs2[e - 1] = part.astype(BF16)
            send(cs2.at[e - 1], cz.at[3 - e], cz_s.at[e - 1], cz_r.at[3 - e], dev(0, 0, e, 0))


    def input_grad():
        for slot in range(3):
            arrived(cz.at[slot], cz_r.at[slot])
        total = tot[...] + cz[0].astype(F32) + cz[1].astype(F32) + cz[2].astype(F32)
        low = total.astype(BF16)
        for b in range(6):
            gi_ref[:, b * 512:(b + 1) * 512] = dot(low[:, b * 128:(b + 1) * 128], comp_ref[...], NT).astype(BF16)

    def transpose_grads():
        for i in range(8):
            og_t[:, i * 128:(i + 1) * 128] = og_all[i].T

    send_grads()
    comp_copy.wait()
    w_copy.wait()
    compute_half(0, 0)
    send_x_only(1)
    send_relay(1, 2)
    send_relay(0, 1)
    send_x_only(0)
    send_relay(0, -1)
    send_relay(1, 1)
    reduce_slot(0)
    send_relay(0, 2)
    send_grads_on()
    compute_half(0, 1)
    gather(3)
    send_relay(1, -1)
    gather(2)
    compute_half(1, 0)
    pass_grads(0, 1)
    pass_grads(0, 0)
    pass_x(1, 1)
    pass_x(0, 2)
    reduce_slot(1)
    compute_half(1, 1)
    pass_x(1, 2)
    gather(5)
    pass_x(0, 0)
    gather(6)
    pass_grads(1, 1)
    pass_grads(1, 0)
    send_y(0, 2)
    pass_x(0, 1)
    other_z(1, 1)
    gather(4)
    compute_half(2, 0)
    compute_half(2, 1)
    send_y(0, -1)
    send_y(0, 1)
    gather(7)
    reduce_slot(3)
    compute_half(3, 0)
    reduce_slot(5)
    compute_half(3, 1)
    own_z(0, 2)
    pass_x(1, 0)
    send_y(1, 2)
    other_z(0, 0)
    reduce_slot(4)
    reduce_slot(6)
    other_z(1, 2)
    send_y(1, -1)
    other_z(0, 1)
    send_y(1, 1)
    reduce_slot(2)
    reduce_slot(7)
    other_z(1, 0)
    x_only(0, 0)
    transpose_grads()
    other_z(0, 2)
    own_z(0, 3)
    own_z(1, 2)
    x_only(1, 0)
    own_z(0, 1)
    near_z(1, 7)
    x_only(0, 1)
    near_z(0, 5)
    pass_core(0, 0, 0)
    near_z(0, 4)
    x_only(1, 1)
    codes_z(2)
    pass_core(0, 0, 1)
    pass_core(0, 1, 0)
    for cp in own_copies:
        cp.wait()
    weight_grad(mine_k(0))
    near_z(0, 3)
    near_z(0, 2)
    pass_core(1, 0, 1)
    codes_z(1)
    codes_z(3)
    own_z(1, 1)
    own_z(1, 3)
    near_z(0, 7)
    near_z(1, 3)
    pass_core(0, 1, 1)
    near_z(1, 6)
    near_z(1, 5)
    weight_grad(mine_k(1))
    pass_core(1, 1, 0)
    near_z(0, 6)
    near_z(1, 2)
    pass_core(1, 0, 0)
    partner_grad(0, 0)
    near_z(1, 4)
    pass_core(1, 1, 1)
    weight_grad(near_k(1))
    partner_grad(0, 1)
    weight_grad(near_k(0))
    codes_z(0)
    partner_grad(1, 0)
    partner_grad(1, 1)
    input_grad()

    for cp in sends:
        cp.wait_send()
    for dy in range(4):
        pltpu.make_async_copy(csend.at[dy], csend.at[dy], cx_s.at[dy]).wait()


def on_device(out_grad, hidden, weight, compress, feedback):
    dma = pltpu.SemaphoreType.DMA
    vmem = pl.BlockSpec(memory_space=pltpu.VMEM)
    hbm = pl.BlockSpec(memory_space=pltpu.HBM)
    return pl.pallas_call(
        body,
        out_shape=(
            OUT((64, 3072), BF16),
            OUT((3072, 384), BF16),
            OUT((1, 1024, 3072), BF16),
        ),
        in_specs=[hbm] * 5,
        out_specs=(vmem, vmem, vmem),
        scratch_shapes=[
            pltpu.VMEM((8, 128, 384), BF16),
            pltpu.VMEM((384, 1024), BF16),
            pltpu.VMEM((512, 128), BF16),
            pltpu.VMEM((2, 3, 64, CHUNK), BF16),
            pltpu.VMEM((3072, 384), BF16),
            pltpu.VMEM((8, 128, 3072), BF16),
            pltpu.VMEM((8, 8, 128, CHUNK), BF16),
            pltpu.VMEM((8, 128, 768), F32),
            pltpu.VMEM((8, 64, 768), F32),
            pltpu.VMEM((4, 64, 768), BF16),
            pltpu.VMEM((4, 64, 768), BF16),
            pltpu.VMEM((4, 64, 768), F32),
            pltpu.VMEM((3, 64, 768), BF16),
            pltpu.VMEM((3, 64, 768), BF16),
            pltpu.VMEM((64, 768), F32),
            dma((7,)), dma((8,)), dma((2, 2)), dma((2, 2)), dma((2, 8)), dma((2, 8)), dma((2, 3)), dma((2, 3)),
            dma((2, 2, 2)), dma((2, 2, 2)), dma((2, 3, 2)), dma((2, 3, 2)), dma((2, 8)), dma((2, 8)),
            dma((2, 2, 2)), dma((2, 2, 2)),
            dma((8,)), dma((8,)), dma((4,)), dma((4,)), dma((3,)), dma((3,)),
            dma, dma, dma, dma((8,)), dma((8,)),
        ],
        compiler_params=pltpu.CompilerParams(
            collective_id=0, has_side_effects=True, vmem_limit_bytes=36 * 2**20
        ),
        cost_estimate=pl.CostEstimate(flops=6_500_000_000, bytes_accessed=25_000_000, transcendentals=0),
    )(*[pltpu.with_memory_space_constraint(a, pltpu.HBM) for a in (out_grad, hidden, weight, compress, feedback)])


OUT = pltpu.VMEM


def solution(mesh):
    return jax.shard_map(
        on_device,
        mesh=mesh,
        in_specs=(P("row", "col"), P("row", None), P("row", "col"), P(), P("col", None, "row")),
        out_specs=(P("col", "row"), P("row", "col"), P("col", None, "row")),
        check_vma=False,
    )
```

```python
import jax
import jax.numpy as jnp
from jax import lax
from jax.experimental import pallas as pl
from jax.experimental.pallas import tpu as pltpu
from jax.sharding import PartitionSpec as P

MESH = pl.DeviceIdType.MESH
NT = (((1,), (1,)), ((), ()))
NN = (((1,), (0,)), ((), ()))
F32 = jnp.float32
BF16 = jnp.bfloat16

SLOTS = [(0, 0), (1, 0), (0, 1), (0, 3), (0, 2), (1, 1), (1, 3), (1, 2)]
POS = {slot: i for i, slot in enumerate(SLOTS)}
CHUNK = 384
DIRECT = ((1, 1), (1, 3))


def dot(a, b, dims):
    return lax.dot_general(a, b, dims, preferred_element_type=F32)


def body(og_ref, hidden, weight, compress, feedback, gi_ref, gw_ref, nf_ref,
         og_all, og_t, comp_ref, rel, w_buf, fbuf, hid, cbuf, pbuf, csend, cx, ksum, cs2, cz, tot,
         g_s, g_r, gf_s, gf_r, hy_s, hy_r, rl_s, rl_r, xo_s, xo_r, hx_s, hx_r, hz_s, hz_r, hc_s, hc_r,
         p_s, p_r, cx_s, cx_r, cz_s, cz_r, comp_sem, og_sem, w_sem, f_sem, own_sem):
    row = lax.axis_index("row")
    col = lax.axis_index("col")
    x_lo, y = row // 4, row % 4
    core, z, x_hi = col % 2, (col // 2) % 4, col // 8
    x = x_hi * 2 + x_lo

    def dev(dx, dy, dz, dc):
        xx, yy, zz, cc = (x + dx + 4) % 4, (y + dy + 4) % 4, (z + dz + 4) % 4, (core + dc) % 2
        return ((xx % 2) * 4 + yy, ((xx // 2) * 4 + zz) * 2 + cc)

    x_pair = 1 - 2 * x_lo
    par = z % 2

    def z_step(t):
        return (1 - 2 * ((t + core) % 2)) * (1 - 2 * par)

    barrier = pltpu.get_barrier_semaphore()
    peers = [dev(0, 1, 0, 0), dev(0, -1, 0, 0), dev(0, 2, 0, 0), dev(1, 0, 0, 0), dev(-1, 0, 0, 0), dev(2, 0, 0, 0),
             dev(0, 0, 1, 0), dev(0, 0, -1, 0), dev(0, 0, 2, 0), dev(0, 0, 0, 1)]
    for peer in peers:
        pl.semaphore_signal(barrier, inc=1, device_id=peer, device_id_type=MESH)

    def row_of(slot):
        dx, dy = slot
        xl = x_lo if dx == 0 else 1 - x_lo
        return xl * 4 + (y + dy) % 4

    comp_copy = pltpu.make_async_copy(compress, comp_ref, comp_sem)
    comp_copy.start()
    og_copy = pltpu.make_async_copy(og_ref, og_all.at[0], og_sem)
    og_copy.start()
    w_copy = pltpu.make_async_copy(weight, w_buf, w_sem)
    w_copy.start()
    f_copies = []
    for i, slot in enumerate(SLOTS):
        start = pl.multiple_of(row_of(slot) * 128, 128)
        cp = pltpu.make_async_copy(feedback.at[0, pl.ds(start, 128), :], fbuf.at[i], f_sem.at[i])
        cp.start()
        f_copies.append(cp)
    own_copies = []
    for k in range(8):
        start = pl.multiple_of(row * 3072 + k * CHUNK, 128)
        cp = pltpu.make_async_copy(hidden.at[:, pl.ds(start, CHUNK)], hid.at[k, 0], own_sem.at[k])
        cp.start()
        own_copies.append(cp)

    pl.semaphore_wait(barrier, len(peers))

    sends = []

    def send(src, dst, s_sem, r_sem, to):
        cp = pltpu.make_async_remote_copy(src_ref=src, dst_ref=dst, send_sem=s_sem, recv_sem=r_sem,
                                          device_id=to, device_id_type=MESH)
        cp.start()
        sends.append(cp)
        return cp

    def arrived(dst, sem):
        pltpu.make_async_copy(dst, dst, sem).wait()

    def send_grads():
        og_copy.wait()
        i = POS[1, 0]
        send(og_all.at[0], og_all.at[i], g_s.at[0], g_r.at[i], dev(x_pair, 0, 0, 0))
        for n, a in enumerate((1, -1)):
            i = POS[0, (-a) % 4]
            send(og_all.at[0], og_all.at[i], g_s.at[1 + n], g_r.at[i], dev(0, a, 0, 0))

    def chunk_of(p, t, c):
        return p * 4 + t * 2 + c

    def cols(r, k):
        return pl.ds(pl.multiple_of(r * 3072 + k * CHUNK, 128), CHUNK)

    half = pl.ds(pl.multiple_of(x_hi * 64, 64), 64)

    def send_x_only(t):
        for pp in range(2):
            k = chunk_of((par + pp) % 2, t, core)
            for n, step in enumerate((1, -1)):
                send(hidden.at[half, cols((1 - x_lo) * 4 + y, k)], hid.at[k, 1, half, :], xo_s.at[pp, t, n],
                     xo_r.at[pp, t, x_hi], dev(step, 0, 0, 0))

    def send_relay(t, a):
        k = chunk_of(par, t, core)
        d = (-a) % 4 - 1
        send(hidden.at[half, cols((1 - x_lo) * 4 + (y + a + 4) % 4, k)], rel.at[t, d], rl_s.at[t, d], rl_r.at[t, d],
             dev(0, a, 0, 0))

    def send_y(t, a):
        k = chunk_of(par, t, core)
        i = POS[0, (-a) % 4]
        send(hidden.at[:, cols(x_lo * 4 + (y + a + 4) % 4, k)], hid.at[k, i], hy_s.at[t, i], hy_r.at[t, i],
             dev(0, a, 0, 0))
        if (t, (-a) % 4) in DIRECT:
            k = chunk_of(1 - par, t, core)
            send(hidden.at[:, cols(x_lo * 4 + (y + a + 4) % 4, k)], hid.at[k, i], hz_s.at[t, i], hz_r.at[t, i],
                 dev(0, a, 0, 0))

    def pass_x(t, d):
        k = chunk_of(par, t, core)
        arrived(rel.at[t, d], rl_r.at[t, d])
        for n, step in enumerate((1, -1)):
            send(rel.at[t, d], hid.at[k, POS[1, d + 1], half, :], hx_s.at[t, d, n], hx_r.at[t, d, x_hi],
                 dev(step, 0, 0, 0))

    def send_grads_on():
        i = POS[1, 0]
        arrived(og_all.at[i], g_r.at[i])
        for n, a in enumerate((1, -1)):
            j = POS[1, (-a) % 4]
            send(og_all.at[i], og_all.at[j], g_s.at[4 + n], g_r.at[j], dev(0, a, 0, 0))

    def compute_half(pair, h):
        ia, ib = (2 * pair, 2 * pair + 1) if pair else (h, h)
        if h == 0 or pair == 0:
            f_copies[ia].wait()
        if h == 0 and pair > 0:
            f_copies[ib].wait()
        rows = [pl.multiple_of(row_of(SLOTS[i]) * 128, 128) for i in range(ia, ib + 1)]
        n = ib + 1 - ia

        blocks = range(3 * h, 3 * h + 3) if pair else range(6)
        grads = og_all[ia:ib + 1].reshape(n * 128, 384)
        accs = []
        for b in blocks:
            u = slice(b * 512, b * 512 + 512)
            accs.append(dot(grads, w_buf[u, :], NT) + fbuf[ia:ib + 1, :, u].reshape(n * 128, 512).astype(F32))
        lows = []
        for b, acc in zip(blocks, accs):
            code = dot(acc.astype(BF16), comp_ref[...], NN)
            cbuf[ia:ib + 1, :, b * 128:b * 128 + 128] = code.reshape(n, 128, 128)
            lows.append(code.astype(BF16))
        for b, acc, low in zip(blocks, accs, lows):
            u = slice(b * 512, b * 512 + 512)
            fresh = (acc - dot(low, comp_ref[...], NT)).astype(BF16)
            for j in range(n):
                nf_ref[0, pl.ds(rows[j], 128), u] = fresh[j * 128:j * 128 + 128]
        if h == 0 and pair > 0:
            return
        theirs = pl.ds(pl.multiple_of((1 - core) * 64, 64), 64)
        for i in range(ia, ib + 1):
            send(cbuf.at[i, theirs, :], pbuf.at[i], p_s.at[i], p_r.at[i], dev(0, 0, 0, 1))

    def reduce_slot(i):
        mine = pl.ds(pl.multiple_of(core * 64, 64), 64)
        dx, dy = SLOTS[i]
        arrived(pbuf.at[i], p_r.at[i])
        xl = x_lo if dx == 0 else 1 - x_lo

        @pl.when(xl == x_hi)
        def _():
            ksum[dy] = cbuf[i, mine, :] + pbuf[i]

        @pl.when(xl != x_hi)
        def _():
            csend[dy] = (cbuf[i, mine, :] + pbuf[i]).astype(BF16)
            pltpu.make_async_remote_copy(
                src_ref=csend.at[dy], dst_ref=cx.at[dy], send_sem=cx_s.at[dy], recv_sem=cx_r.at[dy],
                device_id=dev(2, 0, 0, 0), device_id_type=MESH).start()

    halves = (pl.ds(0, 64), pl.ds(64, 64))

    def gather(i):
        dx, dy = SLOTS[i]
        if dy == 2:
            for h in range(2):
                arrived(og_all.at[i, halves[h], :], gf_r.at[dx, h])
        else:
            arrived(og_all.at[i], g_r.at[i])

    def pass_grads(dx, h):
        i, j = POS[dx, 1 + 2 * h], POS[dx, 2]
        send(og_all.at[i, halves[h], :], og_all.at[j, halves[h], :], gf_s.at[dx, h], gf_r.at[dx, h],
             dev(0, 2 * h - 1, 0, 0))

    def mine_k(t):
        return chunk_of(par, t, core)

    def near_k(t):
        return chunk_of(1 - par, t, core)

    def pass_z(t, i):
        k = mine_k(t)
        send(hid.at[k, i], hid.at[k, i], hz_s.at[t, i], hz_r.at[t, i], dev(0, 0, z_step(t), 0))

    def own_z(t, *dys):
        for dy in dys:
            i = POS[0, dy]
            arrived(hid.at[mine_k(t), i], hy_r.at[t, i])
            if (t, dy) not in DIRECT:
                pass_z(t, i)

    def other_z(t, *ds):
        for d in ds:
            i = POS[1, d + 1]
            for q in range(2):
                arrived(hid.at[mine_k(t), i, q * 64:(q + 1) * 64, :], hx_r.at[t, d, q])
            pass_z(t, i)

    def x_only(pp, t):
        k = chunk_of((par + pp) % 2, t, core)
        for q in range(2):
            arrived(hid.at[k, 1, q * 64:(q + 1) * 64, :], xo_r.at[pp, t, q])

    groups = (pl.ds(5, 3), pl.ds(1, 4))

    def pass_core(pp, t, g):
        part = hid.at[chunk_of((par + pp) % 2, t, core), groups[g]]
        send(part, part, hc_s.at[pp, t, g], hc_r.at[pp, t, g], dev(0, 0, 0, 1))

    def near_z(t, *slots):
        for i in slots:
            arrived(hid.at[near_k(t), i], hz_r.at[t, i])

    def weight_grad(k):
        out = dot(og_t[...], hid[k].reshape(1024, CHUNK), NN)
        gw_ref[pl.ds(pl.multiple_of(k * CHUNK, CHUNK), CHUNK), :] = out.T.astype(BF16)

    def partner_grad(pp, t):
        k = chunk_of((par + pp) % 2, t, 1 - core)
        for g in range(2):
            arrived(hid.at[k, groups[g]], hc_r.at[pp, t, g])
        weight_grad(k)

    def codes_z(e):
        dy = (z + e - y + 4) % 4
        arrived(cx.at[dy], cx_r.at[dy])
        part = ksum[dy] + cx[dy].astype(F32)
        if e == 0:
            tot[...] = part
        else:
            cs2[e - 1] = part.astype(BF16)
            send(cs2.at[e - 1], cz.at[3 - e], cz_s.at[e - 1], cz_r.at[3 - e], dev(0, 0, e, 0))


    def input_grad():
        for slot in range(3):
            arrived(cz.at[slot], cz_r.at[slot])
        total = tot[...] + cz[0].astype(F32) + cz[1].astype(F32) + cz[2].astype(F32)
        low = total.astype(BF16)
        for b in range(6):
            gi_ref[:, b * 512:(b + 1) * 512] = dot(low[:, b * 128:(b + 1) * 128], comp_ref[...], NT).astype(BF16)

    def transpose_grads():
        for i in range(8):
            og_t[:, i * 128:(i + 1) * 128] = og_all[i].T

    send_grads()
    send_x_only(0)
    send_relay(0, 1)
    send_x_only(1)
    send_relay(0, -1)
    send_relay(1, -1)
    send_relay(1, 1)
    send_relay(1, 2)
    comp_copy.wait()
    w_copy.wait()
    compute_half(0, 0)
    send_grads_on()
    gather(3)
    gather(2)
    pass_grads(0, 0)
    compute_half(1, 0)
    pass_grads(0, 1)
    send_relay(0, 2)
    pass_x(0, 0)
    pass_x(0, 2)
    compute_half(1, 1)
    pass_x(1, 0)
    pass_x(1, 2)
    compute_half(0, 1)
    pass_x(1, 1)
    reduce_slot(0)
    gather(5)
    gather(6)
    pass_grads(1, 0)
    other_z(0, 0)
    pass_grads(1, 1)
    send_y(0, 2)
    reduce_slot(1)
    send_y(0, -1)
    send_y(0, 1)
    other_z(0, 2)
    gather(4)
    compute_half(2, 0)
    compute_half(2, 1)
    send_y(1, 2)
    x_only(1, 1)
    pass_x(0, 1)
    reduce_slot(3)
    other_z(1, 2)
    gather(7)
    compute_half(3, 0)
    other_z(1, 0)
    reduce_slot(5)
    compute_half(3, 1)
    other_z(1, 1)
    own_z(0, 2)
    reduce_slot(4)
    send_y(1, 1)
    send_y(1, -1)
    reduce_slot(2)
    other_z(0, 1)
    reduce_slot(6)
    transpose_grads()
    near_z(0, 6)
    x_only(0, 1)
    own_z(0, 1)
    reduce_slot(7)
    own_z(0, 3)
    x_only(0, 0)
    near_z(1, 6)
    pass_core(0, 1, 0)
    own_z(1, 2)
    codes_z(2)
    pass_core(0, 0, 0)
    pass_core(0, 0, 1)
    codes_z(0)
    x_only(1, 0)
    near_z(0, 7)
    codes_z(1)
    own_z(1, 1)
    near_z(1, 5)
    codes_z(3)
    own_z(1, 3)
    near_z(0, 4)
    for cp in own_copies:
        cp.wait()
    weight_grad(mine_k(0))
    near_z(0, 5)
    near_z(1, 3)
    near_z(1, 7)
    near_z(1, 2)
    pass_core(1, 1, 0)
    pass_core(0, 1, 1)
    near_z(0, 3)
    partner_grad(0, 0)
    near_z(0, 2)
    near_z(1, 4)
    pass_core(1, 1, 1)
    pass_core(1, 0, 1)
    pass_core(1, 0, 0)
    weight_grad(near_k(0))
    weight_grad(near_k(1))
    weight_grad(mine_k(1))
    partner_grad(0, 1)
    partner_grad(1, 1)
    partner_grad(1, 0)
    input_grad()

    for cp in sends:
        cp.wait_send()
    for dy in range(4):
        pltpu.make_async_copy(csend.at[dy], csend.at[dy], cx_s.at[dy]).wait()


def on_device(out_grad, hidden, weight, compress, feedback):
    dma = pltpu.SemaphoreType.DMA
    vmem = pl.BlockSpec(memory_space=pltpu.VMEM)
    hbm = pl.BlockSpec(memory_space=pltpu.HBM)
    return pl.pallas_call(
        body,
        out_shape=(
            OUT((64, 3072), BF16),
            OUT((3072, 384), BF16),
            OUT((1, 1024, 3072), BF16),
        ),
        in_specs=[hbm] * 5,
        out_specs=(vmem, vmem, vmem),
        scratch_shapes=[
            pltpu.VMEM((8, 128, 384), BF16),
            pltpu.VMEM((384, 1024), BF16),
            pltpu.VMEM((512, 128), BF16),
            pltpu.VMEM((2, 3, 64, CHUNK), BF16),
            pltpu.VMEM((3072, 384), BF16),
            pltpu.VMEM((8, 128, 3072), BF16),
            pltpu.VMEM((8, 8, 128, CHUNK), BF16),
            pltpu.VMEM((8, 128, 768), F32),
            pltpu.VMEM((8, 64, 768), F32),
            pltpu.VMEM((4, 64, 768), BF16),
            pltpu.VMEM((4, 64, 768), BF16),
            pltpu.VMEM((4, 64, 768), F32),
            pltpu.VMEM((3, 64, 768), BF16),
            pltpu.VMEM((3, 64, 768), BF16),
            pltpu.VMEM((64, 768), F32),
            dma((7,)), dma((8,)), dma((2, 2)), dma((2, 2)), dma((2, 8)), dma((2, 8)), dma((2, 3)), dma((2, 3)),
            dma((2, 2, 2)), dma((2, 2, 2)), dma((2, 3, 2)), dma((2, 3, 2)), dma((2, 8)), dma((2, 8)),
            dma((2, 2, 2)), dma((2, 2, 2)),
            dma((8,)), dma((8,)), dma((4,)), dma((4,)), dma((3,)), dma((3,)),
            dma, dma, dma, dma((8,)), dma((8,)),
        ],
        compiler_params=pltpu.CompilerParams(
            collective_id=0, has_side_effects=True, vmem_limit_bytes=36 * 2**20
        ),
        cost_estimate=pl.CostEstimate(flops=6_500_000_000, bytes_accessed=25_000_000, transcendentals=0),
    )(*[pltpu.with_memory_space_constraint(a, pltpu.HBM) for a in (out_grad, hidden, weight, compress, feedback)])


OUT = pltpu.VMEM


def solution(mesh):
    return jax.shard_map(
        on_device,
        mesh=mesh,
        in_specs=(P("row", "col"), P("row", None), P("row", "col"), P(), P("col", None, "row")),
        out_specs=(P("col", "row"), P("row", "col"), P("col", None, "row")),
        check_vma=False,
    )
```

```python
import jax
import jax.numpy as jnp
from jax import lax
from jax.experimental import pallas as pl
from jax.experimental.pallas import tpu as pltpu
from jax.sharding import PartitionSpec as P

MESH = pl.DeviceIdType.MESH
NT = (((1,), (1,)), ((), ()))
NN = (((1,), (0,)), ((), ()))
F32 = jnp.float32
BF16 = jnp.bfloat16

SLOTS = [(0, 0), (1, 0), (0, 1), (0, 3), (0, 2), (1, 1), (1, 3), (1, 2)]
POS = {slot: i for i, slot in enumerate(SLOTS)}
CHUNK = 384
DIRECT = ((1, 1), (1, 3))


def dot(a, b, dims):
    return lax.dot_general(a, b, dims, preferred_element_type=F32)


def body(og_ref, hidden, weight, compress, feedback, gi_ref, gw_ref, nf_ref,
         og_all, og_t, comp_ref, rel, w_buf, fbuf, hid, cbuf, pbuf, csend, cx, ksum, cs2, cz, tot,
         g_s, g_r, gf_s, gf_r, hy_s, hy_r, rl_s, rl_r, xo_s, xo_r, hx_s, hx_r, hz_s, hz_r, hc_s, hc_r,
         p_s, p_r, cx_s, cx_r, cz_s, cz_r, comp_sem, og_sem, w_sem, f_sem, own_sem):
    row = lax.axis_index("row")
    col = lax.axis_index("col")
    x_lo, y = row // 4, row % 4
    core, z, x_hi = col % 2, (col // 2) % 4, col // 8
    x = x_hi * 2 + x_lo

    def dev(dx, dy, dz, dc):
        xx, yy, zz, cc = (x + dx + 4) % 4, (y + dy + 4) % 4, (z + dz + 4) % 4, (core + dc) % 2
        return ((xx % 2) * 4 + yy, ((xx // 2) * 4 + zz) * 2 + cc)

    x_pair = 1 - 2 * x_lo
    par = z % 2

    def z_step(t):
        return (1 - 2 * ((t + core) % 2)) * (1 - 2 * par)

    barrier = pltpu.get_barrier_semaphore()
    peers = [dev(0, 1, 0, 0), dev(0, -1, 0, 0), dev(0, 2, 0, 0), dev(1, 0, 0, 0), dev(-1, 0, 0, 0), dev(2, 0, 0, 0),
             dev(0, 0, 1, 0), dev(0, 0, -1, 0), dev(0, 0, 2, 0), dev(0, 0, 0, 1)]
    for peer in peers:
        pl.semaphore_signal(barrier, inc=1, device_id=peer, device_id_type=MESH)

    def row_of(slot):
        dx, dy = slot
        xl = x_lo if dx == 0 else 1 - x_lo
        return xl * 4 + (y + dy) % 4

    comp_copy = pltpu.make_async_copy(compress, comp_ref, comp_sem)
    comp_copy.start()
    og_copy = pltpu.make_async_copy(og_ref, og_all.at[0], og_sem)
    og_copy.start()
    w_copy = pltpu.make_async_copy(weight, w_buf, w_sem)
    w_copy.start()
    f_copies = []
    for i, slot in enumerate(SLOTS):
        start = pl.multiple_of(row_of(slot) * 128, 128)
        cp = pltpu.make_async_copy(feedback.at[0, pl.ds(start, 128), :], fbuf.at[i], f_sem.at[i])
        cp.start()
        f_copies.append(cp)
    own_copies = []
    for k in range(8):
        start = pl.multiple_of(row * 3072 + k * CHUNK, 128)
        cp = pltpu.make_async_copy(hidden.at[:, pl.ds(start, CHUNK)], hid.at[k, 0], own_sem.at[k])
        cp.start()
        own_copies.append(cp)

    pl.semaphore_wait(barrier, len(peers))

    sends = []

    def send(src, dst, s_sem, r_sem, to):
        cp = pltpu.make_async_remote_copy(src_ref=src, dst_ref=dst, send_sem=s_sem, recv_sem=r_sem,
                                          device_id=to, device_id_type=MESH)
        cp.start()
        sends.append(cp)
        return cp

    def arrived(dst, sem):
        pltpu.make_async_copy(dst, dst, sem).wait()

    def send_grads():
        og_copy.wait()
        i = POS[1, 0]
        send(og_all.at[0], og_all.at[i], g_s.at[0], g_r.at[i], dev(x_pair, 0, 0, 0))
        for n, a in enumerate((1, -1)):
            i = POS[0, (-a) % 4]
            send(og_all.at[0], og_all.at[i], g_s.at[1 + n], g_r.at[i], dev(0, a, 0, 0))

    def chunk_of(p, t, c):
        return p * 4 + t * 2 + c

    def cols(r, k):
        return pl.ds(pl.multiple_of(r * 3072 + k * CHUNK, 128), CHUNK)

    half = pl.ds(pl.multiple_of(x_hi * 64, 64), 64)

    def send_x_only(t):
        for pp in range(2):
            k = chunk_of((par + pp) % 2, t, core)
            for n, step in enumerate((1, -1)):
                send(hidden.at[half, cols((1 - x_lo) * 4 + y, k)], hid.at[k, 1, half, :], xo_s.at[pp, t, n],
                     xo_r.at[pp, t, x_hi], dev(step, 0, 0, 0))

    def send_relay(t, a):
        k = chunk_of(par, t, core)
        d = (-a) % 4 - 1
        send(hidden.at[half, cols((1 - x_lo) * 4 + (y + a + 4) % 4, k)], rel.at[t, d], rl_s.at[t, d], rl_r.at[t, d],
             dev(0, a, 0, 0))

    def send_y(t, a):
        k = chunk_of(par, t, core)
        i = POS[0, (-a) % 4]
        send(hidden.at[:, cols(x_lo * 4 + (y + a + 4) % 4, k)], hid.at[k, i], hy_s.at[t, i], hy_r.at[t, i],
             dev(0, a, 0, 0))
        if (t, (-a) % 4) in DIRECT:
            k = chunk_of(1 - par, t, core)
            send(hidden.at[:, cols(x_lo * 4 + (y + a + 4) % 4, k)], hid.at[k, i], hz_s.at[t, i], hz_r.at[t, i],
                 dev(0, a, 0, 0))

    def pass_x(t, d):
        k = chunk_of(par, t, core)
        arrived(rel.at[t, d], rl_r.at[t, d])
        for n, step in enumerate((1, -1)):
            send(rel.at[t, d], hid.at[k, POS[1, d + 1], half, :], hx_s.at[t, d, n], hx_r.at[t, d, x_hi],
                 dev(step, 0, 0, 0))

    def send_grads_on():
        i = POS[1, 0]
        arrived(og_all.at[i], g_r.at[i])
        for n, a in enumerate((1, -1)):
            j = POS[1, (-a) % 4]
            send(og_all.at[i], og_all.at[j], g_s.at[4 + n], g_r.at[j], dev(0, a, 0, 0))

    def compute_half(pair, h):
        ia, ib = (2 * pair, 2 * pair + 1) if pair else (h, h)
        if h == 0 or pair == 0:
            f_copies[ia].wait()
        if h == 0 and pair > 0:
            f_copies[ib].wait()
        rows = [pl.multiple_of(row_of(SLOTS[i]) * 128, 128) for i in range(ia, ib + 1)]
        n = ib + 1 - ia

        blocks = range(3 * h, 3 * h + 3) if pair else range(6)
        grads = og_all[ia:ib + 1].reshape(n * 128, 384)
        accs = []
        for b in blocks:
            u = slice(b * 512, b * 512 + 512)
            accs.append(dot(grads, w_buf[u, :], NT) + fbuf[ia:ib + 1, :, u].reshape(n * 128, 512).astype(F32))
        lows = []
        for b, acc in zip(blocks, accs):
            code = dot(acc.astype(BF16), comp_ref[...], NN)
            cbuf[ia:ib + 1, :, b * 128:b * 128 + 128] = code.reshape(n, 128, 128)
            lows.append(code.astype(BF16))
        for b, acc, low in zip(blocks, accs, lows):
            u = slice(b * 512, b * 512 + 512)
            fresh = (acc - dot(low, comp_ref[...], NT)).astype(BF16)
            for j in range(n):
                nf_ref[0, pl.ds(rows[j], 128), u] = fresh[j * 128:j * 128 + 128]
        if h == 0 and pair > 0:
            return
        theirs = pl.ds(pl.multiple_of((1 - core) * 64, 64), 64)
        for i in range(ia, ib + 1):
            send(cbuf.at[i, theirs, :], pbuf.at[i], p_s.at[i], p_r.at[i], dev(0, 0, 0, 1))

    def reduce_slot(i):
        mine = pl.ds(pl.multiple_of(core * 64, 64), 64)
        dx, dy = SLOTS[i]
        arrived(pbuf.at[i], p_r.at[i])
        xl = x_lo if dx == 0 else 1 - x_lo

        @pl.when(xl == x_hi)
        def _():
            ksum[dy] = cbuf[i, mine, :] + pbuf[i]

        @pl.when(xl != x_hi)
        def _():
            csend[dy] = (cbuf[i, mine, :] + pbuf[i]).astype(BF16)
            pltpu.make_async_remote_copy(
                src_ref=csend.at[dy], dst_ref=cx.at[dy], send_sem=cx_s.at[dy], recv_sem=cx_r.at[dy],
                device_id=dev(2, 0, 0, 0), device_id_type=MESH).start()

    halves = (pl.ds(0, 64), pl.ds(64, 64))

    def gather(i):
        dx, dy = SLOTS[i]
        if dy == 2:
            for h in range(2):
                arrived(og_all.at[i, halves[h], :], gf_r.at[dx, h])
        else:
            arrived(og_all.at[i], g_r.at[i])

    def pass_grads(dx, h):
        i, j = POS[dx, 1 + 2 * h], POS[dx, 2]
        send(og_all.at[i, halves[h], :], og_all.at[j, halves[h], :], gf_s.at[dx, h], gf_r.at[dx, h],
             dev(0, 2 * h - 1, 0, 0))

    def mine_k(t):
        return chunk_of(par, t, core)

    def near_k(t):
        return chunk_of(1 - par, t, core)

    def pass_z(t, i):
        k = mine_k(t)
        send(hid.at[k, i], hid.at[k, i], hz_s.at[t, i], hz_r.at[t, i], dev(0, 0, z_step(t), 0))

    def own_z(t, *dys):
        for dy in dys:
            i = POS[0, dy]
            arrived(hid.at[mine_k(t), i], hy_r.at[t, i])
            if (t, dy) not in DIRECT:
                pass_z(t, i)

    def other_z(t, *ds):
        for d in ds:
            i = POS[1, d + 1]
            for q in range(2):
                arrived(hid.at[mine_k(t), i, q * 64:(q + 1) * 64, :], hx_r.at[t, d, q])
            pass_z(t, i)

    def x_only(pp, t):
        k = chunk_of((par + pp) % 2, t, core)
        for q in range(2):
            arrived(hid.at[k, 1, q * 64:(q + 1) * 64, :], xo_r.at[pp, t, q])

    groups = (pl.ds(5, 3), pl.ds(1, 4))

    def pass_core(pp, t, g):
        part = hid.at[chunk_of((par + pp) % 2, t, core), groups[g]]
        send(part, part, hc_s.at[pp, t, g], hc_r.at[pp, t, g], dev(0, 0, 0, 1))

    def near_z(t, *slots):
        for i in slots:
            arrived(hid.at[near_k(t), i], hz_r.at[t, i])

    def weight_grad(k):
        out = dot(og_t[...], hid[k].reshape(1024, CHUNK), NN)
        gw_ref[pl.ds(pl.multiple_of(k * CHUNK, CHUNK), CHUNK), :] = out.T.astype(BF16)

    def partner_grad(pp, t):
        k = chunk_of((par + pp) % 2, t, 1 - core)
        for g in range(2):
            arrived(hid.at[k, groups[g]], hc_r.at[pp, t, g])
        weight_grad(k)

    def codes_z(e):
        dy = (z + e - y + 4) % 4
        arrived(cx.at[dy], cx_r.at[dy])
        part = ksum[dy] + cx[dy].astype(F32)
        if e == 0:
            tot[...] = part
        else:
            cs2[e - 1] = part.astype(BF16)
            send(cs2.at[e - 1], cz.at[3 - e], cz_s.at[e - 1], cz_r.at[3 - e], dev(0, 0, e, 0))


    def input_grad():
        for slot in range(3):
            arrived(cz.at[slot], cz_r.at[slot])
        total = tot[...] + cz[0].astype(F32) + cz[1].astype(F32) + cz[2].astype(F32)
        low = total.astype(BF16)
        for b in range(6):
            gi_ref[:, b * 512:(b + 1) * 512] = dot(low[:, b * 128:(b + 1) * 128], comp_ref[...], NT).astype(BF16)

    def transpose_grads():
        for i in range(8):
            og_t[:, i * 128:(i + 1) * 128] = og_all[i].T

    send_grads()
    send_relay(0, -1)
    send_relay(1, -1)
    send_x_only(1)
    send_relay(0, 1)
    comp_copy.wait()
    w_copy.wait()
    compute_half(0, 0)
    send_relay(1, 1)
    send_relay(1, 2)
    send_relay(0, 2)
    send_x_only(0)
    send_grads_on()
    gather(2)
    send_y(0, 2)
    compute_half(0, 1)
    pass_x(0, 2)
    pass_x(1, 0)
    gather(3)
    pass_x(1, 2)
    pass_grads(0, 1)
    compute_half(1, 0)
    pass_x(0, 0)
    compute_half(1, 1)
    pass_x(0, 1)
    gather(6)
    gather(5)
    pass_grads(1, 0)
    pass_grads(1, 1)
    pass_x(1, 1)
    other_z(0, 2)
    send_y(0, 1)
    pass_grads(0, 0)
    reduce_slot(3)
    send_y(0, -1)
    reduce_slot(1)
    send_y(1, 1)
    own_z(0, 2)
    reduce_slot(2)
    other_z(1, 2)
    send_y(1, 2)
    gather(7)
    compute_half(3, 0)
    compute_half(3, 1)
    other_z(0, 1)
    gather(4)
    compute_half(2, 0)
    own_z(0, 1)
    reduce_slot(7)
    compute_half(2, 1)
    reduce_slot(0)
    reduce_slot(6)
    own_z(0, 3)
    other_z(0, 0)
    x_only(1, 0)
    send_y(1, -1)
    near_z(0, 6)
    own_z(1, 3)
    reduce_slot(4)
    reduce_slot(5)
    x_only(1, 1)
    x_only(0, 0)
    near_z(1, 3)
    other_z(1, 1)
    own_z(1, 2)
    near_z(1, 6)
    other_z(1, 0)
    pass_core(0, 0, 1)
    codes_z(3)
    x_only(0, 1)
    transpose_grads()
    pass_core(0, 0, 0)
    pass_core(0, 1, 0)
    codes_z(1)
    near_z(0, 3)
    near_z(0, 2)
    codes_z(2)
    own_z(1, 1)
    near_z(1, 7)
    pass_core(0, 1, 1)
    near_z(0, 7)
    near_z(0, 5)
    near_z(1, 2)
    for cp in own_copies:
        cp.wait()
    weight_grad(mine_k(0))
    near_z(1, 4)
    pass_core(1, 1, 1)
    near_z(0, 4)
    pass_core(1, 0, 1)
    pass_core(1, 0, 0)
    near_z(1, 5)
    pass_core(1, 1, 0)
    weight_grad(near_k(1))
    weight_grad(mine_k(1))
    partner_grad(0, 1)
    codes_z(0)
    partner_grad(0, 0)
    partner_grad(1, 0)
    partner_grad(1, 1)
    weight_grad(near_k(0))
    input_grad()

    for cp in sends:
        cp.wait_send()
    for dy in range(4):
        pltpu.make_async_copy(csend.at[dy], csend.at[dy], cx_s.at[dy]).wait()


def on_device(out_grad, hidden, weight, compress, feedback):
    dma = pltpu.SemaphoreType.DMA
    vmem = pl.BlockSpec(memory_space=pltpu.VMEM)
    hbm = pl.BlockSpec(memory_space=pltpu.HBM)
    return pl.pallas_call(
        body,
        out_shape=(
            OUT((64, 3072), BF16),
            OUT((3072, 384), BF16),
            OUT((1, 1024, 3072), BF16),
        ),
        in_specs=[hbm] * 5,
        out_specs=(vmem, vmem, vmem),
        scratch_shapes=[
            pltpu.VMEM((8, 128, 384), BF16),
            pltpu.VMEM((384, 1024), BF16),
            pltpu.VMEM((512, 128), BF16),
            pltpu.VMEM((2, 3, 64, CHUNK), BF16),
            pltpu.VMEM((3072, 384), BF16),
            pltpu.VMEM((8, 128, 3072), BF16),
            pltpu.VMEM((8, 8, 128, CHUNK), BF16),
            pltpu.VMEM((8, 128, 768), F32),
            pltpu.VMEM((8, 64, 768), F32),
            pltpu.VMEM((4, 64, 768), BF16),
            pltpu.VMEM((4, 64, 768), BF16),
            pltpu.VMEM((4, 64, 768), F32),
            pltpu.VMEM((3, 64, 768), BF16),
            pltpu.VMEM((3, 64, 768), BF16),
            pltpu.VMEM((64, 768), F32),
            dma((7,)), dma((8,)), dma((2, 2)), dma((2, 2)), dma((2, 8)), dma((2, 8)), dma((2, 3)), dma((2, 3)),
            dma((2, 2, 2)), dma((2, 2, 2)), dma((2, 3, 2)), dma((2, 3, 2)), dma((2, 8)), dma((2, 8)),
            dma((2, 2, 2)), dma((2, 2, 2)),
            dma((8,)), dma((8,)), dma((4,)), dma((4,)), dma((3,)), dma((3,)),
            dma, dma, dma, dma((8,)), dma((8,)),
        ],
        compiler_params=pltpu.CompilerParams(
            collective_id=0, has_side_effects=True, vmem_limit_bytes=36 * 2**20
        ),
        cost_estimate=pl.CostEstimate(flops=6_500_000_000, bytes_accessed=25_000_000, transcendentals=0),
    )(*[pltpu.with_memory_space_constraint(a, pltpu.HBM) for a in (out_grad, hidden, weight, compress, feedback)])


OUT = pltpu.VMEM


def solution(mesh):
    return jax.shard_map(
        on_device,
        mesh=mesh,
        in_specs=(P("row", "col"), P("row", None), P("row", "col"), P(), P("col", None, "row")),
        out_specs=(P("col", "row"), P("row", "col"), P("col", None, "row")),
        check_vma=False,
    )
```
